512 devices in a mesh: dp: 128 (over z, y, core), query: 4 (over x).
Axes of the slice: x: 4, y: 8, z: 8, core: 2. Of those that a mesh axis runs over, the one named last changes fastest.
Arguments:
- x_act: bfloat16 [65536, 8192], P('dp', 'query'), may hold values from -18 to 18
- g_out: bfloat16 [65536, 8192], P('dp', 'query'), may hold values from -6 to 6
- proj_in: bfloat16 [8192, 64], P('query'), may hold values from -0.16572815 to 0.16572815
- proj_out: bfloat16 [8192, 64], P('query'), may hold values from -0.16572815 to 0.16572815
- doc_lengths: int32 [128, 16], P('dp'), may hold values from 1 to 256, 512 in all within a row
- query_grads: bfloat16 [4096, 2048], P('dp', 'query'), may hold values from -0.09375 to 0.09375
Outputs:
- scores: float32 [2048, 2048], P('dp', 'query')
The draws below stay inside these ranges and needn't reach their ends.
Inputs may be any that keep to these rules, and one draw needn't show every extreme that they name: `doc_lengths`: each row sums to 512, and its largest entry is exactly 256.
All inputs are finite; a program needn't handle non-finite values.
Results may differ from the reference program's by a relative error of at most 0.0088.
Values may be sent and summed in bfloat16 or wider, within the bound.
No kernel may reach another device: no remote copies, remote signals or barrier semaphores. Data moves between devices by JAX's collectives and lax.ppermute only.
A program may use at most 64 MiB of HBM per device.

```python
import math
import jax
import jax.numpy as jnp
import numpy as np
from jax import lax

D = 8192
RANK = 64
T_DEV = 512
DOC_SLOTS = 16
MAX_LEN = 256
FEAT = 4096
TOKENS = 65536
BLOCKS = 128
DOCS = 2048
QUERIES = 2048


def mixed_projection(key, row_total):
    sample = jnp.clip(jax.random.normal(key, (row_total, RANK), jnp.float32), -5.0, 5.0)
    scales = jnp.exp(jax.random.uniform(jax.random.fold_in(key, 7), (RANK,), jnp.float32, -0.7, 0.7))
    blended = sample + 0.7 * jnp.roll(sample, 1, axis=1)
    return (blended * scales[None, :] / jnp.sqrt(1.49 * row_total)).astype(jnp.bfloat16)


def draw_proj_in(key, part):
    key = jax.random.fold_in(key, 11)
    return mixed_projection(key, D)


def draw_proj_out(key, part):
    key = jax.random.fold_in(key, 23)
    return mixed_projection(key, D)


def draw_x_act(key, part):
    key = jax.random.fold_in(key, 3)
    sample = jnp.clip(jax.random.normal(key, (TOKENS, D), jnp.float32), -6.0, 6.0)
    growth = jnp.exp(jnp.log(3.0) * jnp.arange(TOKENS, dtype=jnp.float32) / TOKENS)
    return (sample * growth[:, None]).astype(jnp.bfloat16)


def levels(stream_key, dims, cuts, smallest, high):
    def one(axis_at, blocks):
        heights = jax.random.uniform(jax.random.fold_in(jax.random.fold_in(stream_key, 6), axis_at), (blocks,), jnp.float32, smallest / len(cuts), high / len(cuts))
        return jnp.repeat(jnp.exp(heights), dims[axis_at] // blocks).reshape((-1,) + (1,) * (len(dims) - axis_at - 1))

    loudness = one(*cuts[0])
    for cut in cuts[1:]:
        loudness = loudness * one(*cut)
    return loudness


def length_profile(count, total, limit, slope):
    loads = [(1 << 20) // math.isqrt(grade ** slope) + 1 for grade in range(2, count + 1)]
    spare, holding = total - limit - (count - 1), [1] * (count - 1)
    while spare > 0:
        free = [i for i in range(count - 1) if holding[i] < limit]
        pool, left = sum([loads[i] for i in free]), spare
        for i in free:
            more = min(limit - holding[i], max(1, left * loads[i] // pool), spare)
            holding[i] = holding[i] + more
            spare = spare - more
    return np.array([limit] + holding)


def uneven(stream_key, number_of, total, bound, lean):
    if number_of == 2:
        one = jax.random.randint(stream_key, (), max(1, total - bound), min(bound, total - 1) + 1)
        return jnp.stack([one, total - one])
    sizes = jnp.asarray(length_profile(number_of, total, bound, lean), jnp.int32)
    couples = (number_of - 1) // 2
    source_of, taker = sizes[1:1 + 2 * couples:2], sizes[2:2 + 2 * couples:2]
    room = jnp.minimum(source_of - 1, bound - taker)
    moved = jax.random.randint(jax.random.fold_in(stream_key, 1), (couples,), 0, 1 << 20) % (room + 1)
    sizes = sizes.at[1:1 + 2 * couples:2].set(source_of - moved).at[2:2 + 2 * couples:2].set(taker + moved)
    return sizes[jax.random.permutation(jax.random.fold_in(stream_key, 2), number_of)]


def noise(stream_key, extent, scale, reach, shards=(), held_as=jnp.bfloat16):
    loudness = levels(stream_key, extent, shards, -0.22, 0.18) if shards else 1.0
    entries = jax.random.normal(stream_key, extent, jnp.float32) * scale * loudness
    return jnp.minimum(jnp.maximum(entries, -reach), reach).astype(held_as)


def setup_inputs(seed: int = 0) -> dict:
    splits = jax.random.split(jax.random.key(seed), 7)
    return {
        "x_act": draw_x_act(jax.random.fold_in(splits[6], 71), 0),
        "g_out": noise(splits[1], (TOKENS, D), 1.0, 6.0, ((0, 128), (1, 4))),
        "proj_in": draw_proj_in(jax.random.fold_in(splits[6], 71), 0),
        "proj_out": draw_proj_out(jax.random.fold_in(splits[6], 71), 0),
        "doc_lengths": jax.vmap(lambda own: uneven(own, DOC_SLOTS, T_DEV, MAX_LEN, 2))(jax.random.split(splits[4], BLOCKS)).reshape((BLOCKS, DOC_SLOTS)).astype(jnp.int32),
        "query_grads": noise(splits[5], (FEAT, QUERIES), FEAT ** -0.5, 0.09375, ((0, 128), (1, 4))),
    }


highest = lax.Precision.HIGHEST

def damped_inverse(gram_matrix):
    matrix_order = gram_matrix.shape[0]
    identity = jnp.eye(matrix_order, dtype=jnp.float32)
    damping = 0.1 * jnp.trace(gram_matrix) / matrix_order + 1e-05
    cholesky_factor = jnp.linalg.cholesky(gram_matrix + damping * identity)
    inverse_root = jax.scipy.linalg.solve_triangular(cholesky_factor, identity, lower=True)
    return jnp.dot(inverse_root.T, inverse_root, precision=highest)

def document_sums(input_block, grad_block, lengths):
    total_rows = input_block.shape[0]
    slot_count = lengths.shape[0]
    low_rank = input_block.shape[1]
    finish = jnp.cumsum(lengths).astype(jnp.int32)
    begins = (finish - lengths).astype(jnp.int32)
    places = jnp.arange(total_rows, dtype=jnp.int32)[:, None]
    member = ((places >= begins[None, :]) & (places < finish[None, :])).astype(jnp.float32)
    weighted = (member[:, :, None] * grad_block.astype(jnp.float32)[:, None, :]).reshape(total_rows, slot_count * low_rank)
    doc_sums = jnp.einsum('tk,tb->kb', weighted, input_block.astype(jnp.float32), precision=highest)
    return doc_sums.reshape(slot_count, low_rank, low_rank) / lengths.astype(jnp.float32)[:, None, None]

def reference(x_act, g_out, proj_in, proj_out, doc_lengths, query_grads):
    input_proj = jnp.dot(x_act.astype(jnp.float32), proj_in.astype(jnp.float32), preferred_element_type=jnp.float32).astype(jnp.bfloat16)
    grad_proj = jnp.dot(g_out.astype(jnp.float32), proj_out.astype(jnp.float32), preferred_element_type=jnp.float32).astype(jnp.bfloat16)
    gram_input = jnp.dot(input_proj.T.astype(jnp.float32), input_proj.astype(jnp.float32), preferred_element_type=jnp.float32) / TOKENS
    gram_grad = jnp.dot(grad_proj.T.astype(jnp.float32), grad_proj.astype(jnp.float32), preferred_element_type=jnp.float32) / TOKENS
    inverse_input = damped_inverse(gram_input)
    inverse_grad = damped_inverse(gram_grad)

    def one_block(pieces):
        return document_sums(pieces[0], pieces[1], pieces[2])
    per_block = lax.map(one_block, (input_proj.reshape(BLOCKS, T_DEV, RANK), grad_proj.reshape(BLOCKS, T_DEV, RANK), doc_lengths))
    doc_grads = per_block.reshape(DOCS, RANK, RANK)
    left_side = jnp.einsum('ac,dcb->dab', inverse_grad, doc_grads, precision=highest)
    conditioned = jnp.einsum('dab,be->dae', left_side, inverse_input, precision=highest)
    flat_docs = conditioned.reshape(DOCS, FEAT).astype(jnp.bfloat16)
    return jnp.dot(flat_docs.astype(jnp.float32), query_grads.astype(jnp.float32), preferred_element_type=jnp.float32)
```

```python
import jax
import jax.numpy as jnp
from jax import lax
from jax.sharding import Mesh
from jax.sharding import PartitionSpec as P

highest = lax.Precision.HIGHEST


def damped_inverse(gram_matrix):
    matrix_order = gram_matrix.shape[0]
    identity = jnp.eye(matrix_order, dtype=jnp.float32)
    damping = 0.1 * jnp.trace(gram_matrix) / matrix_order + 1e-05
    cholesky_factor = jnp.linalg.cholesky(gram_matrix + damping * identity)
    inverse_root = jax.scipy.linalg.solve_triangular(cholesky_factor, identity, lower=True)
    return jnp.dot(inverse_root.T, inverse_root, precision=highest)


def outer_sum(projected):
    return jnp.dot(projected.T, projected, preferred_element_type=jnp.float32)


def exchange_sum(value, axis):
    members = lax.axis_size(axis)
    copies = jnp.broadcast_to(value[None], (members, *value.shape))
    return lax.all_to_all(copies, axis, 0, 0, tiled=True).sum(0)


def document_sums(input_block, grad_block, lengths):
    total_rows = input_block.shape[0]
    slot_count = lengths.shape[0]
    low_rank = input_block.shape[1]
    finish = jnp.cumsum(lengths)
    begins = finish - lengths
    places = jnp.arange(total_rows, dtype=jnp.int32)[:, None]
    member = ((places >= begins[None, :]) & (places < finish[None, :])).astype(jnp.bfloat16)
    weighted = (member[:, :, None] * grad_block[:, None, :]).reshape(
        total_rows, slot_count * low_rank
    )
    doc_sums = jnp.einsum("tk,tb->kb", weighted, input_block, preferred_element_type=jnp.float32)
    return (
        doc_sums.reshape(slot_count, low_rank, low_rank)
        / lengths.astype(jnp.float32)[:, None, None]
    )


def local(x_act, g_out, proj_in, proj_out, doc_lengths, query_grads):
    rank = proj_in.shape[1]
    input_part = jnp.dot(x_act, proj_in, preferred_element_type=jnp.float32)
    grad_part = jnp.dot(g_out, proj_out, preferred_element_type=jnp.float32)
    both_sum = exchange_sum(jnp.concatenate([input_part, grad_part], axis=1), "x")
    both = both_sum.astype(jnp.bfloat16)
    input_proj, grad_proj = both[:, :rank], both[:, rank:]
    grams = jnp.concatenate([outer_sum(input_proj), outer_sum(grad_proj)], axis=1)
    core_count = lax.axis_size("c")
    swap = [(i, (i + 1) % core_count) for i in range(core_count)]
    grams = grams + lax.ppermute(grams, "c", swap)
    grams = exchange_sum(grams, "y")
    grams = exchange_sum(grams, "z")
    total_tokens = x_act.shape[0] * lax.axis_size(("z", "y", "c"))
    grams = grams / total_tokens
    inverse_input = damped_inverse(grams[:, :rank])
    inverse_grad = damped_inverse(grams[:, rank:])
    doc_grads = document_sums(input_proj, grad_proj, doc_lengths[0])
    slot_count = doc_grads.shape[0]
    left_side = jnp.einsum("ac,dcb->dab", inverse_grad, doc_grads, precision=highest)
    conditioned = jnp.einsum("dab,be->dae", left_side, inverse_input, precision=highest)
    flat_docs = conditioned.reshape(slot_count, -1).astype(jnp.bfloat16)
    return jnp.dot(
        flat_docs,
        lax.all_gather(query_grads, ("z", "y", "c"), axis=0, tiled=True),
        preferred_element_type=jnp.float32,
    )


def solution(mesh):
    split = Mesh(mesh.devices.reshape(8, 8, 2, 4), ("z", "y", "c", "x"))
    dp = ("z", "y", "c")
    placed = (
        P(dp, "x"),
        P(dp, "x"),
        P("x", None),
        P("x", None),
        P(dp, None),
        P(dp, "x"),
    )
    return jax.shard_map(
        local, mesh=split, in_specs=placed, out_specs=P(dp, "x"), check_vma=False
    )
```

```python
import jax
import jax.numpy as jnp
from jax import lax
from jax.experimental import pallas as pl
from jax.experimental.pallas import tpu as pltpu
from jax.sharding import PartitionSpec as P

highest = lax.Precision.HIGHEST
f32 = jnp.float32
bf16 = jnp.bfloat16
RING = 8
CORES = 2


def place(z, y, core):
    return ((z % RING) * RING + y % RING) * CORES + core


def step_factors(lowest, steps):
    factors = []
    for _ in range(steps):
        factors.append(2.0 / (1.0 + lowest))
        gap = (1.0 - lowest) / (1.0 + lowest)
        lowest = 1.0 - gap * gap
    return factors


def damped_inverses(grams):
    n = grams.shape[0]
    lane = lax.broadcasted_iota(jnp.int32, (n, 2 * n), 1)
    blocks = jnp.concatenate(
        [jnp.where(lane < n, grams, 0.0), jnp.where(lane >= n, grams, 0.0)], axis=0
    )
    row = lax.broadcasted_iota(jnp.int32, (2 * n, 2 * n), 0)
    col = lax.broadcasted_iota(jnp.int32, (2 * n, 2 * n), 1)
    eye = (row == col).astype(f32)
    diagonal = blocks * eye
    first = jnp.sum(diagonal[:n], keepdims=True)
    second = jnp.sum(diagonal[n:], keepdims=True)
    at_row = lax.broadcasted_iota(jnp.int32, (2 * n, 1), 0)
    trace = jnp.where(at_row < n, first, second)
    damping = 0.1 * trace / n + 1e-05
    shrink = 1.0 / (trace + damping)
    matrix = (blocks + damping * eye) * shrink
    factors = step_factors(1.0 / 642.0, 8)
    head = factors[0]
    guess = (2.0 * head) * eye - (head * head) * matrix
    for factor in factors[1:]:
        product = jnp.dot(matrix, guess, precision=highest, preferred_element_type=f32)
        correction = jnp.dot(guess, product, precision=highest, preferred_element_type=f32)
        guess = (2.0 * factor) * guess - (factor * factor) * correction
    return guess * shrink


def finish(token_share, pieces_ref, own_ref, peer_ref, near_hbm, far_hbm, mine_ref, other_ref, held, by_row, arrived):
    steps = held.shape[1]
    copies = [
        [
            pltpu.make_async_copy(hbm.at[t], held.at[s, t], arrived.at[s, t])
            for t in range(steps)
        ]
        for s, hbm in enumerate((near_hbm, far_hbm))
    ]
    for side in copies:
        for copy in side:
            copy.start()
    me = lax.axis_index("dp")
    core = lax.rem(me, CORES)
    at_y = lax.rem(lax.div(me, CORES), RING)
    at_z = lax.div(me, CORES * RING)
    parity = lax.rem(jnp.where(core == 0, at_y, at_z), 2)
    grams = pieces_ref[0]
    for k in range(1, pieces_ref.shape[0]):
        grams = grams + pieces_ref[k]
    inverses = damped_inverses(grams * token_share)
    n = grams.shape[0]
    half = n // CORES
    fit = 2 * n // half
    docs = CORES * own_ref.shape[1] // n
    left = [
        jnp.dot(inverses[n:, n:], ref[...], precision=highest, preferred_element_type=f32)
        for ref in (own_ref, peer_ref)
    ]
    inverse_input = inverses[:n]
    column = lax.broadcasted_iota(jnp.int32, (n, 2 * n), 1)
    columns = jnp.where(core == 0, inverse_input, pltpu.roll(inverse_input, 2 * n - half, 1))
    columns = jnp.where(column < half, columns, 0.0)
    right = jnp.concatenate(
        [columns] + [pltpu.roll(columns, half * j, 1) for j in range(1, fit)], axis=0
    )
    groups = docs // fit
    stack = jnp.concatenate(
        [side[:, g * fit * n : (g + 1) * fit * n] for side in left for g in range(groups // CORES)],
        axis=0,
    )
    both = jnp.dot(stack, right, precision=highest, preferred_element_type=f32)
    for j in range(fit):
        turned = both if j == 0 else pltpu.roll(both, 2 * n - half * j, 1)
        for g in range(groups):
            by_row[pl.ds(g * fit + j, n, stride=docs), :] = turned[g * n : (g + 1) * n]
    lane = lax.broadcasted_iota(jnp.int32, (docs, 2 * n), 1)
    total = jnp.zeros((docs, mine_ref.shape[1]), f32)
    for s in range(2):
        odd = parity if s == 0 else 1 - parity
        for t in range(steps):
            wide = []
            for first in range(0, RING, fit):
                block = None
                for j in range(fit):
                    k = first + j
                    a = jnp.where(
                        core == 0,
                        (2 * t + k // 4) * RING + 2 * (k % 4) + odd,
                        (2 * t + odd) * RING + k,
                    )
                    rows = by_row[pl.ds(pl.multiple_of(a * docs, docs), docs), :]
                    if j == 0:
                        block = rows
                    else:
                        block = jnp.where(lane < half * j, block, pltpu.roll(rows, half * j, 1))
                wide.append(block.astype(bf16))
            copies[s][t].wait()
            part = held[s, t]
            total += jnp.dot(
                jnp.concatenate(wide, axis=1),
                part.reshape(part.shape[0] * part.shape[1], part.shape[2]),
                preferred_element_type=f32,
            )
    mine_ref[...] = total[: docs // CORES]
    other_ref[...] = total[docs // CORES :]


def scores_of(pieces, own_docs, peer_docs, near, far, token_count):
    rank = pieces.shape[1]
    docs = CORES * own_docs.shape[1] // rank
    columns = near.shape[-1]
    vmem = pl.BlockSpec(memory_space=pltpu.VMEM)
    hbm = pl.BlockSpec(memory_space=pltpu.HBM)
    out = jax.ShapeDtypeStruct((docs // CORES, columns), f32)
    shape = (near.shape[0] // RING, RING, *near.shape[1:])
    return pl.pallas_call(
        lambda *refs: finish(1.0 / token_count, *refs),
        out_shape=(out, out),
        in_specs=[vmem, vmem, vmem, hbm, hbm],
        out_specs=(vmem, vmem),
        scratch_shapes=[
            pltpu.VMEM((2, *shape), bf16),
            pltpu.VMEM((rank * docs, 2 * rank), f32),
            pltpu.SemaphoreType.DMA((2, shape[0])),
        ],
        compiler_params=pltpu.CompilerParams(vmem_limit_bytes=32 * 1024 * 1024),
        cost_estimate=pl.CostEstimate(
            flops=docs * rank * rank * columns,
            bytes_accessed=rank * rank * columns,
            transcendentals=0,
        ),
        name="finish",
    )(pieces, own_docs, peer_docs, near.reshape(shape), far.reshape(shape))


def exchange(value, axis, groups=None):
    members = len(groups[0]) if groups else lax.axis_size(axis)
    copies = jnp.broadcast_to(value[None], (members, *value.shape))
    return lax.all_to_all(copies, axis, 0, 0, axis_index_groups=groups, tiled=True)


def along_y():
    return [[place(z, y, k) for y in range(RING)] for z in range(RING) for k in range(CORES)]


def along_z():
    return [[place(z, y, k) for z in range(RING)] for y in range(RING) for k in range(CORES)]


def core_dependent():
    halves = [range(p, RING, 2) for p in range(2)]
    return [[place(z, y, 0) for z in range(RING) for y in half] for half in halves] + [
        [place(z, y, 1) for z in half for y in range(RING)] for half in halves
    ]


def from_neighbour(value):
    pairs = []
    for z in range(RING):
        for y in range(RING):
            pairs.append((place(z, y ^ 1, 0), place(z, y, 0)))
            pairs.append((place(z ^ 1, y, 1), place(z, y, 1)))
    return lax.ppermute(value, "dp", pairs)


def swap_cores(value):
    count = lax.axis_size("dp")
    return lax.ppermute(value, "dp", [(i, i ^ 1) for i in range(count)])


def outer_sum(projected):
    return jnp.dot(projected.T, projected, preferred_element_type=f32)


def document_sums(input_block, grad_block, lengths):
    total_rows, low_rank = input_block.shape
    slot_count = lengths.shape[0]
    finish_at = jnp.cumsum(lengths)
    begins = finish_at - lengths
    places = jnp.arange(total_rows, dtype=jnp.int32)[:, None]
    member = ((places >= begins[None, :]) & (places < finish_at[None, :])).astype(bf16)
    spread = (member[:, :, None] * input_block[:, None, :]).reshape(
        total_rows, slot_count * low_rank
    )
    sums = jnp.dot(grad_block.T, spread, preferred_element_type=f32)
    return sums / jnp.repeat(lengths.astype(f32), low_rank)[None, :]


def local(x_act, g_out, proj_in, proj_out, doc_lengths, query_grads):
    rank = proj_in.shape[1]
    tokens = x_act.shape[0]
    slots = doc_lengths.shape[1]
    near = exchange(query_grads, "dp", core_dependent())
    far = from_neighbour(near)
    input_part = jnp.dot(x_act, proj_in, preferred_element_type=f32)
    grad_part = jnp.dot(g_out, proj_out, preferred_element_type=f32)
    own = lax.psum(jnp.concatenate([input_part, grad_part], axis=1), "query").astype(bf16)
    lengths = jnp.zeros((16, 2 * rank), bf16).at[0, :slots].set(doc_lengths[0].astype(bf16))
    peer = swap_cores(jnp.concatenate([own, lengths], axis=0))
    peer, peer_lengths = peer[:tokens], peer[tokens, :slots].astype(jnp.int32)
    grams = jnp.concatenate(
        [
            outer_sum(own[:, :rank]) + outer_sum(peer[:, :rank]),
            outer_sum(own[:, rank:]) + outer_sum(peer[:, rank:]),
        ],
        axis=1,
    )
    grams = exchange(grams, "dp", along_y()).sum(0)
    pieces = exchange(grams, "dp", along_z())
    own_docs = document_sums(own[:, :rank], own[:, rank:], doc_lengths[0])
    peer_docs = document_sums(peer[:, :rank], peer[:, rank:], peer_lengths)
    mine, other = scores_of(
        pieces, own_docs, peer_docs, near, far, tokens * lax.axis_size("dp")
    )
    return mine + swap_cores(other)


def solution(mesh):
    placed = (
        P("dp", "query"),
        P("dp", "query"),
        P("query", None),
        P("query", None),
        P("dp", None),
        P("dp", "query"),
    )
    return jax.shard_map(
        local, mesh=mesh, in_specs=placed, out_specs=P("dp", "query"), check_vma=False
    )
```

```python
import jax
import jax.numpy as jnp
from jax import lax
from jax.experimental import pallas as pl
from jax.experimental.pallas import tpu as pltpu
from jax.sharding import PartitionSpec as P

highest = lax.Precision.HIGHEST
early = lax.Precision.HIGH
f32 = jnp.float32
bf16 = jnp.bfloat16
RING = 8
CORES = 2
LENGTH_ROWS = 16


def place(z, y, core):
    return ((z % RING) * RING + y % RING) * CORES + core


def step_factors(lowest, steps):
    factors = []
    for _ in range(steps):
        factors.append(2.0 / (1.0 + lowest))
        gap = (1.0 - lowest) / (1.0 + lowest)
        lowest = 1.0 - gap * gap
    return factors


def damped_inverses(blocks):
    n = blocks.shape[0] // 2
    row = lax.broadcasted_iota(jnp.int32, (2 * n, 2 * n), 0)
    col = lax.broadcasted_iota(jnp.int32, (2 * n, 2 * n), 1)
    eye = (row == col).astype(f32)
    diagonal = blocks * eye
    first = jnp.sum(diagonal[:n], keepdims=True)
    second = jnp.sum(diagonal[n:], keepdims=True)
    at_row = lax.broadcasted_iota(jnp.int32, (2 * n, 1), 0)
    trace = jnp.where(at_row < n, first, second)
    damping = 0.1 * trace / n + 1e-05
    shrink = 1.0 / (trace + damping)
    matrix = (blocks + damping * eye) * shrink
    factors = step_factors(1.0 / 642.0, 7)
    miss = eye - factors[0] * matrix
    guess = factors[0] * (eye + miss)
    for factor in factors[1:]:
        square = jnp.dot(miss, miss, precision=early, preferred_element_type=f32)
        miss = (1.0 - factor) * eye + factor * square
        product = jnp.dot(guess, miss, precision=early, preferred_element_type=f32)
        guess = factor * (guess + product)
    product = jnp.dot(matrix, guess, precision=highest, preferred_element_type=f32)
    guess = 2.0 * guess - jnp.dot(guess, product, precision=highest, preferred_element_type=f32)
    return guess * shrink


def folded_grams(own_ref, peer_ref, copies_ref):
    tokens = own_ref.shape[0] - LENGTH_ROWS
    across = (((0,), (0,)), ((), ()))
    own, peer = own_ref[:tokens], peer_ref[:tokens]
    both = lax.dot_general(own, own, across, preferred_element_type=f32) + lax.dot_general(
        peer, peer, across, preferred_element_type=f32
    )
    n = both.shape[0] // 2
    h, q = n // 2, n // 4
    lane = lax.broadcasted_iota(jnp.int32, (h, 2 * n), 1)
    top = jnp.where(lane < n, both[:h], both[n : n + h])
    low = jnp.where(lane < n, both[h:n], both[n + h :])
    low = jnp.where(lax.rem(lane[:q], n) >= h, low[:q], pltpu.roll(low[q:], 2 * n - h, 1))
    folded = jnp.concatenate([top, low], axis=0)
    for k in range(copies_ref.shape[0]):
        copies_ref[k] = folded


def unfolded(folded):
    n = folded.shape[1] // 2
    h = n // 2
    lane = lax.broadcasted_iota(jnp.int32, (h, 2 * n), 1)
    top, low = folded[:h], folded[h:]
    low = jnp.concatenate([low, pltpu.roll(low, h, 1)], axis=0)
    first, second = lane < n, lane >= n
    right = lax.rem(lane, n) >= h
    upper = jnp.concatenate(
        [
            jnp.where(first, top, 0.0),
            jnp.where(first & right, low, 0.0),
            jnp.where(second, top, 0.0),
            jnp.where(second & right, low, 0.0),
        ],
        axis=0,
    )
    none = jnp.zeros_like(top)
    corners = jnp.concatenate(
        [
            jnp.where(first & right, top, 0.0),
            none,
            jnp.where(second & right, top, 0.0),
            none,
        ],
        axis=0,
    )
    return upper + corners.T


def summed(pieces_ref):
    total = pieces_ref[0]
    for k in range(1, pieces_ref.shape[0]):
        total = total + pieces_ref[k]
    return total


def sum_and_copy(pieces_ref, copies_ref):
    total = summed(pieces_ref)
    for k in range(copies_ref.shape[0]):
        copies_ref[k] = total


def document_means(sent, slots):
    tokens = sent.shape[0] - LENGTH_ROWS
    both, lengths = sent[:tokens], sent[tokens:]
    n = both.shape[1] // 2
    wide = slots * n
    slot = lax.broadcasted_iota(jnp.int32, (2 * n, wide), 0)
    document = lax.broadcasted_iota(jnp.int32, (2 * n, wide), 1) // n
    begins = jnp.dot(
        lengths, (slot < document).astype(f32).astype(bf16), preferred_element_type=f32
    )[:1]
    length = jnp.dot(
        lengths, (slot == document).astype(f32).astype(bf16), preferred_element_type=f32
    )[:1]
    ends = begins + length
    inputs = both.astype(f32)
    lane = lax.broadcasted_iota(jnp.int32, inputs.shape, 1)
    twice = jnp.where(lane < n, inputs, pltpu.roll(inputs, n, 1))
    four = jnp.concatenate([twice, twice], axis=1)
    at = lax.broadcasted_iota(jnp.int32, four.shape, 0).astype(f32)
    means = []
    step = four.shape[1]
    for k in range(0, wide, step):
        member = (at >= begins[:, k : k + step]) & (at < ends[:, k : k + step])
        spread = jnp.where(member, four, 0.0).astype(bf16)
        sums = lax.dot_general(both, spread, (((0,), (0,)), ((), ())), preferred_element_type=f32)
        means.append(sums[n:] / length[:, k : k + step])
    return jnp.concatenate(means, axis=1)


def finish(token_share, slots, pieces_ref, own_hbm, peer_hbm, near_hbm, far_hbm, mine_ref, other_ref, held, tokens_held, by_row, arrived, tokens_arrived):
    tokens_copies = [
        pltpu.make_async_copy(hbm, tokens_held.at[s], tokens_arrived.at[s])
        for s, hbm in enumerate((own_hbm, peer_hbm))
    ]
    for copy in tokens_copies:
        copy.start()
    steps = held.shape[1]
    copies = [
        [
            pltpu.make_async_copy(hbm.at[t], held.at[s, t], arrived.at[s, t])
            for t in range(steps)
        ]
        for s, hbm in enumerate((near_hbm, far_hbm))
    ]
    for side in copies:
        for copy in side:
            copy.start()
    me = lax.axis_index("dp")
    core = lax.rem(me, CORES)
    parity = lax.rem(lax.div(me, CORES), 2)
    means = []
    for s in range(CORES):
        tokens_copies[s].wait()
        means.append(document_means(tokens_held[s], slots))
    inverses = damped_inverses(unfolded(summed(pieces_ref)) * token_share)
    n = inverses.shape[0] // 2
    half = n // CORES
    fit = 2 * n // half
    docs = CORES * slots
    left = [
        jnp.dot(inverses[n:, n:], side, precision=highest, preferred_element_type=f32)
        for side in means
    ]
    inverse_input = inverses[:n]
    column = lax.broadcasted_iota(jnp.int32, (n, 2 * n), 1)
    columns = jnp.where(core == 0, inverse_input, pltpu.roll(inverse_input, 2 * n - half, 1))
    columns = jnp.where(column < half, columns, 0.0)
    right = jnp.concatenate(
        [columns] + [pltpu.roll(columns, half * j, 1) for j in range(1, fit)], axis=0
    )
    groups = docs // fit
    stack = jnp.concatenate(
        [side[:, g * fit * n : (g + 1) * fit * n] for side in left for g in range(groups // CORES)],
        axis=0,
    )
    both = jnp.dot(stack, right, precision=highest, preferred_element_type=f32)
    for j in range(fit):
        turned = both if j == 0 else pltpu.roll(both, 2 * n - half * j, 1)
        for g in range(groups):
            by_row[pl.ds(g * fit + j, n, stride=docs), :] = turned[g * n : (g + 1) * n]
    lane = lax.broadcasted_iota(jnp.int32, (docs, 2 * n), 1)
    total = jnp.zeros((docs, mine_ref.shape[1]), f32)
    for s in range(2):
        odd = parity if s == 0 else 1 - parity
        for t in range(steps):
            wide = []
            for first in range(0, RING, fit):
                block = None
                for j in range(fit):
                    k = first + j
                    a = (2 * t + k // 4) * RING + 2 * (k % 4) + odd
                    rows = by_row[pl.ds(pl.multiple_of(a * docs, docs), docs), :]
                    if j == 0:
                        block = rows
                    else:
                        block = jnp.where(lane < half * j, block, pltpu.roll(rows, half * j, 1))
                wide.append(block.astype(bf16))
            copies[s][t].wait()
            part = held[s, t]
            total += jnp.dot(
                jnp.concatenate(wide, axis=1),
                part.reshape(part.shape[0] * part.shape[1], part.shape[2]),
                preferred_element_type=f32,
            )
    mine_ref[...] = total[: docs // CORES]
    other_ref[...] = total[docs // CORES :]


def scores_of(pieces, own, peer, near, far, slots, token_count):
    rank = own.shape[1] // 2
    docs = CORES * slots
    columns = near.shape[-1]
    vmem = pl.BlockSpec(memory_space=pltpu.VMEM)
    hbm = pl.BlockSpec(memory_space=pltpu.HBM)
    out = jax.ShapeDtypeStruct((slots, columns), f32)
    shape = (near.shape[0] // RING, RING, *near.shape[1:])
    return pl.pallas_call(
        lambda *refs: finish(1.0 / token_count, slots, *refs),
        out_shape=(out, out),
        in_specs=[vmem, hbm, hbm, hbm, hbm],
        out_specs=(vmem, vmem),
        scratch_shapes=[
            pltpu.VMEM((2, *shape), bf16),
            pltpu.VMEM((CORES, *own.shape), bf16),
            pltpu.VMEM((rank * docs, 2 * rank), f32),
            pltpu.SemaphoreType.DMA((2, shape[0])),
            pltpu.SemaphoreType.DMA((CORES,)),
        ],
        compiler_params=pltpu.CompilerParams(vmem_limit_bytes=32 * 1024 * 1024),
        cost_estimate=pl.CostEstimate(
            flops=docs * rank * rank * columns,
            bytes_accessed=rank * rank * columns,
            transcendentals=0,
        ),
        name="finish",
    )(pieces, own, peer, near.reshape(shape), far.reshape(shape))


def in_vmem(kernel, out_shape, name, *operands):
    vmem = pl.BlockSpec(memory_space=pltpu.VMEM)
    return pl.pallas_call(
        kernel,
        out_shape=jax.ShapeDtypeStruct(out_shape, f32),
        in_specs=[vmem] * len(operands),
        out_specs=vmem,
        compiler_params=pltpu.CompilerParams(vmem_limit_bytes=16 * 1024 * 1024),
        name=name,
    )(*operands)


def spread(value, members):
    return jnp.broadcast_to(value[None], (members, *value.shape))


def send(copies, groups):
    return lax.all_to_all(copies, "dp", 0, 0, axis_index_groups=groups, tiled=True)


def along_y():
    return [[place(z, y, k) for y in range(RING)] for z in range(RING) for k in range(CORES)]


def along_z():
    return [[place(z, y, k) for z in range(RING)] for y in range(RING) for k in range(CORES)]


def every_second():
    return [
        [place(z, y, k) for z in range(RING) for y in range(p, RING, 2)]
        for p in range(2)
        for k in range(CORES)
    ]


def from_neighbour(value):
    pairs = [
        (place(z, y + side, k), place(z, y, k))
        for z in range(RING)
        for y in range(RING)
        for k, side in ((0, 1), (1, -1))
    ]
    return lax.ppermute(value, "dp", pairs)


def swap_cores(value):
    count = lax.axis_size("dp")
    return lax.ppermute(value, "dp", [(i, i ^ 1) for i in range(count)])


def local(x_act, g_out, proj_in, proj_out, doc_lengths, query_grads):
    rank = proj_in.shape[1]
    tokens = x_act.shape[0]
    slots = doc_lengths.shape[1]
    groups = every_second()
    near = send(spread(query_grads, len(groups[0])), groups)
    input_part = jnp.dot(x_act, proj_in, preferred_element_type=f32)
    grad_part = jnp.dot(g_out, proj_out, preferred_element_type=f32)
    lengths = jnp.where(lax.axis_index("query") == 0, doc_lengths, 0).astype(f32)
    lengths = jnp.pad(lengths, ((0, LENGTH_ROWS - 1), (0, 2 * rank - slots)))
    parts = jnp.concatenate([jnp.concatenate([input_part, grad_part], axis=1), lengths], axis=0)
    own = lax.psum(parts, "query").astype(bf16)
    peer = swap_cores(own)
    folded = (RING, rank * 3 // 4, 2 * rank)
    copies = in_vmem(folded_grams, folded, "grams", own, peer)
    near, copies = lax.optimization_barrier((near, copies))
    copies = in_vmem(sum_and_copy, folded, "between", send(copies, along_y()))
    near, copies = lax.optimization_barrier((near, copies))
    far = from_neighbour(near)
    pieces = send(copies, along_z())
    mine, other = scores_of(
        pieces, own, peer, near, far, slots, tokens * lax.axis_size("dp")
    )
    return mine + swap_cores(other)


def solution(mesh):
    placed = (
        P("dp", "query"),
        P("dp", "query"),
        P("query", None),
        P("query", None),
        P("dp", None),
        P("dp", "query"),
    )
    return jax.shard_map(
        local, mesh=mesh, in_specs=placed, out_specs=P("dp", "query"), check_vma=False
    )
```

```python
import jax
import jax.numpy as jnp
from jax import lax
from jax.experimental import pallas as pl
from jax.experimental.pallas import tpu as pltpu
from jax.sharding import PartitionSpec as P

highest = lax.Precision.HIGHEST
early = lax.Precision.HIGH
f32 = jnp.float32
bf16 = jnp.bfloat16
RING = 8
CORES = 2
LENGTH_ROWS = 16


def place(z, y, core):
    return ((z % RING) * RING + y % RING) * CORES + core


def step_factors(lowest, steps):
    factors = []
    for _ in range(steps):
        factors.append(2.0 / (1.0 + lowest))
        gap = (1.0 - lowest) / (1.0 + lowest)
        lowest = 1.0 - gap * gap
    return factors


def damped_inverses(blocks):
    n = blocks.shape[0] // 2
    row = lax.broadcasted_iota(jnp.int32, (2 * n, 2 * n), 0)
    col = lax.broadcasted_iota(jnp.int32, (2 * n, 2 * n), 1)
    eye = (row == col).astype(f32)
    diagonal = blocks * eye
    first = jnp.sum(diagonal[:n], keepdims=True)
    second = jnp.sum(diagonal[n:], keepdims=True)
    at_row = lax.broadcasted_iota(jnp.int32, (2 * n, 1), 0)
    trace = jnp.where(at_row < n, first, second)
    damping = 0.1 * trace / n + 1e-05
    shrink = 1.0 / (trace + damping)
    matrix = (blocks + damping * eye) * shrink
    factors = step_factors(1.0 / 642.0, 7)
    miss = eye - factors[0] * matrix
    guess = factors[0] * (eye + miss)
    for factor in factors[1:]:
        square = jnp.dot(miss, miss, precision=early, preferred_element_type=f32)
        miss = (1.0 - factor) * eye + factor * square
        product = jnp.dot(guess, miss, precision=early, preferred_element_type=f32)
        guess = factor * (guess + product)
    product = jnp.dot(matrix, guess, precision=highest, preferred_element_type=f32)
    guess = 2.0 * guess - jnp.dot(guess, product, precision=highest, preferred_element_type=f32)
    return guess * shrink


def folded_grams(own_ref, peer_ref, copies_ref):
    tokens = own_ref.shape[0] - LENGTH_ROWS
    across = (((0,), (0,)), ((), ()))
    own, peer = own_ref[:tokens], peer_ref[:tokens]
    both = lax.dot_general(own, own, across, preferred_element_type=f32) + lax.dot_general(
        peer, peer, across, preferred_element_type=f32
    )
    n = both.shape[0] // 2
    h, q = n // 2, n // 4
    lane = lax.broadcasted_iota(jnp.int32, (h, 2 * n), 1)
    top = jnp.where(lane < n, both[:h], both[n : n + h])
    low = jnp.where(lane < n, both[h:n], both[n + h :])
    low = jnp.where(lax.rem(lane[:q], n) >= h, low[:q], pltpu.roll(low[q:], 2 * n - h, 1))
    folded = jnp.concatenate([top, low], axis=0)
    for k in range(copies_ref.shape[0]):
        copies_ref[k] = folded


def unfolded(folded):
    n = folded.shape[1] // 2
    h = n // 2
    lane = lax.broadcasted_iota(jnp.int32, (h, 2 * n), 1)
    top, low = folded[:h], folded[h:]
    low = jnp.concatenate([low, pltpu.roll(low, h, 1)], axis=0)
    first, second = lane < n, lane >= n
    right = lax.rem(lane, n) >= h
    upper = jnp.concatenate(
        [
            jnp.where(first, top, 0.0),
            jnp.where(first & right, low, 0.0),
            jnp.where(second, top, 0.0),
            jnp.where(second & right, low, 0.0),
        ],
        axis=0,
    )
    none = jnp.zeros_like(top)
    corners = jnp.concatenate(
        [
            jnp.where(first & right, top, 0.0),
            none,
            jnp.where(second & right, top, 0.0),
            none,
        ],
        axis=0,
    )
    return upper + corners.T


def summed(pieces_ref):
    total = pieces_ref[0]
    for k in range(1, pieces_ref.shape[0]):
        total = total + pieces_ref[k]
    return total


def sum_and_copy(pieces_ref, copies_ref):
    total = summed(pieces_ref)
    for k in range(copies_ref.shape[0]):
        copies_ref[k] = total


def document_means(sent, slots):
    tokens = sent.shape[0] - LENGTH_ROWS
    both, lengths = sent[:tokens], sent[tokens:]
    n = both.shape[1] // 2
    wide = slots * n
    slot = lax.broadcasted_iota(jnp.int32, (2 * n, wide), 0)
    document = lax.broadcasted_iota(jnp.int32, (2 * n, wide), 1) // n
    begins = jnp.dot(
        lengths, (slot < document).astype(f32).astype(bf16), preferred_element_type=f32
    )[:1]
    length = jnp.dot(
        lengths, (slot == document).astype(f32).astype(bf16), preferred_element_type=f32
    )[:1]
    ends = begins + length
    inputs = both.astype(f32)
    lane = lax.broadcasted_iota(jnp.int32, inputs.shape, 1)
    twice = jnp.where(lane < n, inputs, pltpu.roll(inputs, n, 1))
    four = jnp.concatenate([twice, twice], axis=1)
    at = lax.broadcasted_iota(jnp.int32, four.shape, 0).astype(f32)
    means = []
    step = four.shape[1]
    for k in range(0, wide, step):
        member = (at >= begins[:, k : k + step]) & (at < ends[:, k : k + step])
        spread = jnp.where(member, four, 0.0).astype(bf16)
        sums = lax.dot_general(both, spread, (((0,), (0,)), ((), ())), preferred_element_type=f32)
        means.append(sums[n:] / length[:, k : k + step])
    return jnp.concatenate(means, axis=1)


def write_document_means(slots, own_ref, peer_ref, means_ref):
    for s, ref in enumerate((own_ref, peer_ref)):
        means_ref[s] = document_means(ref[...], slots)


def finish(token_share, slots, pieces_ref, means_ref, near_hbm, far_hbm, mine_ref, other_ref, held, by_row, arrived):
    steps = held.shape[1]
    copies = [
        [
            pltpu.make_async_copy(hbm.at[t], held.at[s, t], arrived.at[s, t])
            for t in range(steps)
        ]
        for s, hbm in enumerate((near_hbm, far_hbm))
    ]
    for side in copies:
        for copy in side:
            copy.start()
    me = lax.axis_index("dp")
    core = lax.rem(me, CORES)
    parity = lax.rem(lax.div(me, CORES), 2)
    inverses = damped_inverses(unfolded(summed(pieces_ref)) * token_share)
    n = inverses.shape[0] // 2
    half = n // CORES
    fit = 2 * n // half
    docs = CORES * slots
    left = [
        jnp.dot(inverses[n:, n:], means_ref[s], precision=highest, preferred_element_type=f32)
        for s in range(CORES)
    ]
    inverse_input = inverses[:n]
    column = lax.broadcasted_iota(jnp.int32, (n, 2 * n), 1)
    columns = jnp.where(core == 0, inverse_input, pltpu.roll(inverse_input, 2 * n - half, 1))
    columns = jnp.where(column < half, columns, 0.0)
    right = jnp.concatenate(
        [columns] + [pltpu.roll(columns, half * j, 1) for j in range(1, fit)], axis=0
    )
    groups = docs // fit
    stack = jnp.concatenate(
        [side[:, g * fit * n : (g + 1) * fit * n] for side in left for g in range(groups // CORES)],
        axis=0,
    )
    both = jnp.dot(stack, right, precision=highest, preferred_element_type=f32)
    for j in range(fit):
        turned = both if j == 0 else pltpu.roll(both, 2 * n - half * j, 1)
        for g in range(groups):
            by_row[pl.ds(g * fit + j, n, stride=docs), :] = turned[g * n : (g + 1) * n]
    lane = lax.broadcasted_iota(jnp.int32, (docs, 2 * n), 1)
    total = jnp.zeros((docs, mine_ref.shape[1]), f32)
    for s in range(2):
        odd = parity if s == 0 else 1 - parity
        for t in range(steps):
            wide = []
            for first in range(0, RING, fit):
                block = None
                for j in range(fit):
                    k = first + j
                    a = k * RING + 2 * t + odd
                    rows = by_row[pl.ds(pl.multiple_of(a * docs, docs), docs), :]
                    if j == 0:
                        block = rows
                    else:
                        block = jnp.where(lane < half * j, block, pltpu.roll(rows, half * j, 1))
                wide.append(block.astype(bf16))
            copies[s][t].wait()
            part = held[s, t]
            total += jnp.dot(
                jnp.concatenate(wide, axis=1),
                part.reshape(part.shape[0] * part.shape[1], part.shape[2]),
                preferred_element_type=f32,
            )
    mine_ref[...] = total[: docs // CORES]
    other_ref[...] = total[docs // CORES :]


def scores_of(pieces, doc_means, near, far, slots, token_count):
    rank = doc_means.shape[1]
    docs = CORES * slots
    columns = near.shape[-1]
    vmem = pl.BlockSpec(memory_space=pltpu.VMEM)
    hbm = pl.BlockSpec(memory_space=pltpu.HBM)
    out = jax.ShapeDtypeStruct((slots, columns), f32)
    shape = (near.shape[0] // RING, RING, *near.shape[1:])
    return pl.pallas_call(
        lambda *refs: finish(1.0 / token_count, slots, *refs),
        out_shape=(out, out),
        in_specs=[vmem, vmem, hbm, hbm],
        out_specs=(vmem, vmem),
        scratch_shapes=[
            pltpu.VMEM((2, *shape), bf16),
            pltpu.VMEM((rank * docs, 2 * rank), f32),
            pltpu.SemaphoreType.DMA((2, shape[0])),
        ],
        compiler_params=pltpu.CompilerParams(vmem_limit_bytes=32 * 1024 * 1024),
        cost_estimate=pl.CostEstimate(
            flops=docs * rank * rank * columns,
            bytes_accessed=rank * rank * columns,
            transcendentals=0,
        ),
        name="finish",
    )(pieces, doc_means, near.reshape(shape), far.reshape(shape))


def in_vmem(kernel, out_shape, name, *operands):
    vmem = pl.BlockSpec(memory_space=pltpu.VMEM)
    return pl.pallas_call(
        kernel,
        out_shape=jax.ShapeDtypeStruct(out_shape, f32),
        in_specs=[vmem] * len(operands),
        out_specs=vmem,
        compiler_params=pltpu.CompilerParams(vmem_limit_bytes=16 * 1024 * 1024),
        name=name,
    )(*operands)


def spread(value, members):
    return jnp.broadcast_to(value[None], (members, *value.shape))


def send(copies, groups):
    return lax.all_to_all(copies, "dp", 0, 0, axis_index_groups=groups, tiled=True)


def along_y():
    return [[place(z, y, k) for y in range(RING)] for z in range(RING) for k in range(CORES)]


def along_z():
    return [[place(z, y, k) for z in range(RING)] for y in range(RING) for k in range(CORES)]


def every_second():
    return [
        [place(z, y, k) for y in range(p, RING, 2) for z in range(RING)]
        for p in range(2)
        for k in range(CORES)
    ]


def from_neighbour(value):
    pairs = [
        (place(z, y + side, k), place(z, y, k))
        for z in range(RING)
        for y in range(RING)
        for k, side in ((0, 1), (1, -1))
    ]
    return lax.ppermute(value, "dp", pairs)


def swap_cores(value):
    count = lax.axis_size("dp")
    return lax.ppermute(value, "dp", [(i, i ^ 1) for i in range(count)])


def local(x_act, g_out, proj_in, proj_out, doc_lengths, query_grads):
    rank = proj_in.shape[1]
    tokens = x_act.shape[0]
    slots = doc_lengths.shape[1]
    groups = every_second()
    near = send(spread(query_grads, len(groups[0])), groups)
    input_part = jnp.dot(x_act, proj_in, preferred_element_type=f32)
    grad_part = jnp.dot(g_out, proj_out, preferred_element_type=f32)
    lengths = jnp.where(lax.axis_index("query") == 0, doc_lengths, 0).astype(f32)
    lengths = jnp.pad(lengths, ((0, LENGTH_ROWS - 1), (0, 2 * rank - slots)))
    parts = jnp.concatenate([jnp.concatenate([input_part, grad_part], axis=1), lengths], axis=0)
    own = lax.psum(parts, "query").astype(bf16)
    peer = swap_cores(own)
    folded = (RING, rank * 3 // 4, 2 * rank)
    copies = in_vmem(folded_grams, folded, "grams", own, peer)
    doc_means = in_vmem(
        lambda *refs: write_document_means(slots, *refs),
        (CORES, rank, slots * rank),
        "documents",
        own,
        peer,
    )
    near, doc_means, copies = lax.optimization_barrier((near, doc_means, copies))
    copies = in_vmem(sum_and_copy, folded, "between", send(copies, along_y()))
    near, copies = lax.optimization_barrier((near, copies))
    far = from_neighbour(near)
    pieces = send(copies, along_z())
    mine, other = scores_of(
        pieces, doc_means, near, far, slots, tokens * lax.axis_size("dp")
    )
    return mine + swap_cores(other)


def solution(mesh):
    placed = (
        P("dp", "query"),
        P("dp", "query"),
        P("query", None),
        P("query", None),
        P("dp", None),
        P("dp", "query"),
    )
    return jax.shard_map(
        local, mesh=mesh, in_specs=placed, out_specs=P("dp", "query"), check_vma=False
    )
```
